256 devices in a mesh: rep: 8 (over y, x_hi), loop: 32 (over z, x_lo, core).
Axes of the slice: x: 4 (x_hi: 2, x_lo: 2; x = x_hi * 2 + x_lo), y: 4, z: 8, core: 2. Of those that a mesh axis runs over, the one named last changes fastest.
Arguments:
- interactions: int32 [2, 262144, 1024], P(None, ('rep', 'loop')), may hold values from 0 to 3
- user_factors: float32 [262144, 128], P(('rep', 'loop')), may hold values from -2 to 2
- item_factors: float32 [32768, 128], P('loop'), may hold values from -2 to 2
Outputs:
- user_out: float32 [262144, 128], P(('rep', 'loop'))
- item_out: float32 [32768, 128], P('loop')
The draws below stay inside these ranges and needn't reach their ends.
All inputs are finite; a program needn't handle non-finite values.
Results may differ from the reference program's by a relative error of at most 0.0003.
Values sent between devices are 32-bit elements; how exact they have to be, the bound alone decides.
A program may use at most 64 MiB of HBM per device.

```python
import jax
import jax.numpy as jnp
from jax import lax

R = 128
USERS_DEV = 1024
ITEMS_DEV = 1024
STRATA = 2
USERS = 262144
ITEMS = 32768
N_REP = 8
N_LOOP = 32


def set_ends(entries, stream_key, smallest, top_value):
    index_at = [jax.random.randint(jax.random.fold_in(stream_key, axis), (), 0, length) for axis, length in enumerate(entries.shape)]
    widest = entries.shape.index(max(entries.shape))
    neighbour = index_at[:widest] + [(index_at[widest] + 1) % entries.shape[widest]] + index_at[widest + 1:]
    return entries.at[tuple(index_at)].set(smallest).at[tuple(neighbour)].set(top_value)


def levels(own_key, shape, cuts, smallest, largest):
    level = 1.0
    for axis_at, parts in cuts:
        heights = jax.random.uniform(jax.random.fold_in(jax.random.fold_in(own_key, 6), axis_at), (parts,), jnp.float32, smallest / len(cuts), largest / len(cuts))
        level = level * jnp.repeat(jnp.exp(heights), shape[axis_at] // parts).reshape((-1,) + (1,) * (len(shape) - 1 - axis_at))
    return level


def gaussian(key, dims, deviation, reach, shards=(), held_as=jnp.bfloat16):
    factor_of = levels(key, dims, shards, -0.22, 0.18) if shards else 1.0
    entries = jax.random.normal(key, dims, jnp.float32) * deviation * factor_of
    return jnp.minimum(jnp.maximum(entries, -reach), reach).astype(held_as)


def setup_inputs(seed: int = 0) -> dict:
    splits = jax.random.split(jax.random.key(seed), 4)
    interactions = set_ends(jax.random.randint(splits[0], (STRATA, USERS, ITEMS_DEV), 0, 4), jax.random.fold_in(splits[0], 1), 0, 3).astype(jnp.int32)
    user_factors = gaussian(splits[1], (USERS, R), 0.3, 2.0, ((0, 256),), jnp.float32)
    item_factors = gaussian(splits[2], (ITEMS, R), 0.3, 2.0, ((0, 32),), jnp.float32)
    return {"interactions": interactions, "user_factors": user_factors, "item_factors": item_factors}


ALPHA = 0.5
RATE = 0.01
DECAY = 0.05


def replica_window(args):
    users, counts = args[0], args[1]
    held = args[2]
    hp = lax.Precision.HIGHEST
    for s in range(STRATA):
        tile = counts[s]
        conf = 1.0 + ALPHA * tile.astype(jnp.float32)
        pref = (tile > 0).astype(jnp.float32)
        pred = jnp.einsum('lur,lir->lui', users, held, precision=hp)
        err = conf * (pref - pred)
        new_items = held + RATE * (jnp.einsum('lui,lur->lir', err, users, precision=hp) - DECAY * held)
        users = users + RATE * (jnp.einsum('lui,lir->lur', err, held, precision=hp) - DECAY * users)
        held = new_items
        if s + 1 < STRATA:
            held = jnp.roll(held, 1, axis=0)
    return users, held


def reference(interactions, user_factors, item_factors):
    users = user_factors.reshape(N_REP, N_LOOP, USERS_DEV, R)
    counts = interactions.reshape(STRATA, N_REP, N_LOOP, USERS_DEV, ITEMS_DEV)
    counts = jnp.transpose(counts, (1, 0, 2, 3, 4))
    start = jnp.broadcast_to(item_factors.reshape(1, N_LOOP, ITEMS_DEV, R), (N_REP, N_LOOP, ITEMS_DEV, R))
    new_users, held = lax.map(replica_window, (users, counts, start))
    item_out = jnp.mean(held, axis=0).reshape(ITEMS, R)
    return new_users.reshape(USERS, R), item_out
```

```python
import functools

import jax
import jax.numpy as jnp
from jax import lax
from jax.experimental import pallas as pl
from jax.experimental.pallas import tpu as pltpu
from jax.sharding import PartitionSpec as P

ALPHA = 0.5
RATE = 0.01
DECAY = 0.05
KEEP = 1.0 - RATE * DECAY
STEP = RATE * ALPHA
N = 1024
R = 128
CHUNK = 256
CHUNKS = N // CHUNK
ROWS = 256
REPS = 8
PIECE = CHUNK // REPS
OTHERS = [(2, 1), (1, 1), (3, 1), (2, 0), (0, 1), (1, 0), (3, 0)]
MESH = pl.DeviceIdType.MESH
F32 = jnp.float32
BF16 = jnp.bfloat16
NT = (((1,), (1,)), ((), ()))
NN = (((1,), (0,)), ((), ()))


def split(x):
    hi = x.astype(BF16)
    return hi, (x - hi.astype(F32)).astype(BF16)


def dot(a, b, dims):
    return lax.dot_general(a, b, dims, preferred_element_type=F32)


def kernel(comm, inter, users, items, user_out, item_out, tile, uv, held0, held1, sent0, sent1,
           ucat, utcat, hpred, hnew, ghi, glo, parts, mean,
           in_sem, tile_sem, out_sem, own_sem, ring_send, ring_recv, rs_send, rs_recv, ag_send, ag_recv):
    if comm:
        rep = lax.axis_index("rep")
        loop = lax.axis_index("loop")
        y, xh = rep // 2, rep % 2
        after = (rep, (loop + 1) % 32)
        before = (rep, (loop + 31) % 32)
        ranks_to = [((y + a) % 4) * 2 + (xh + b) % 2 for a, b in OTHERS]
        ranks_from = [((y + 4 - a) % 4) * 2 + (xh + b) % 2 for a, b in OTHERS]
        barrier = pltpu.get_barrier_semaphore()
        pl.semaphore_signal(barrier, inc=1, device_id=before, device_id_type=MESH)
        for k in range(len(OTHERS)):
            pl.semaphore_signal(barrier, inc=1, device_id=(ranks_from[k], loop), device_id_type=MESH)
    else:
        rep = 0

    loads = [pltpu.make_async_copy(users, uv, in_sem.at[0]), pltpu.make_async_copy(items, held0, in_sem.at[1])]
    for c in loads:
        c.start()
    tiles = []
    for s in range(2):
        for c in range(CHUNKS):
            cols = pl.ds(c * CHUNK, CHUNK)
            t = pltpu.make_async_copy(inter.at[s, :, cols], tile.at[s, :, cols], tile_sem.at[s, c])
            t.start()
            tiles.append(t)
    for c in loads:
        c.wait()

    ring = []
    scatter = []
    gather = []
    outs = []
    for s in range(2):
        held = held0 if s == 0 else held1
        sent = sent0 if s == 0 else sent1
        for u in range(N // ROWS):
            rows = pl.ds(u * ROWS, ROWS)
            block = uv[rows, :]
            hi, lo = split(block)
            ucat[rows, 0:R] = hi
            ucat[rows, R:2 * R] = lo
            hi, lo = split(block.T)
            utcat[0:R, rows] = hi
            utcat[R:2 * R, rows] = lo
        for c in range(CHUNKS):
            cols = pl.ds(c * CHUNK, CHUNK)
            if s == 1 and comm:
                ring[c].wait_recv()
            h = held[cols, :]
            hi, lo = split(h)
            hnew[cols, 0:R] = hi
            hnew[cols, R:2 * R] = lo
            hpred[:, 0:R] = hi
            hpred[:, R:2 * R] = hi
            hpred[:, 2 * R:3 * R] = lo
            hpred[:, 3 * R:4 * R] = lo
            tiles[s * CHUNKS + c].wait()
            for u in range(N // ROWS):
                rows = pl.ds(u * ROWS, ROWS)
                uc = ucat[rows, :]
                pred = dot(uc, hpred[:, 0:2 * R], NT) + dot(uc, hpred[:, 2 * R:4 * R], NT)
                t = tile[s, rows, cols].astype(F32)
                hi, lo = split((1.0 / ALPHA + t) * (jnp.minimum(t, 1.0) - pred))
                ghi[rows, cols] = hi
                glo[rows, cols] = lo
            d = dot(utcat[...], ghi[:, cols], NN) + dot(utcat[...], glo[:, cols], NN)
            new = KEEP * h + STEP * (d[0:R] + d[R:2 * R]).T
            sent[cols, :] = new
            if not comm:
                if s == 0:
                    held1[cols, :] = new
                else:
                    o = pltpu.make_async_copy(sent1.at[cols], item_out.at[cols], own_sem.at[c])
                    o.start()
                    outs.append(o)
                continue
            if s == 0:
                if c == 0:
                    pl.semaphore_wait(barrier, 1 + len(OTHERS))
                cp = pltpu.make_async_remote_copy(
                    src_ref=sent0.at[cols], dst_ref=held1.at[cols],
                    send_sem=ring_send.at[c], recv_sem=ring_recv.at[c],
                    device_id=after, device_id_type=MESH)
                cp.start()
                ring.append(cp)
            else:
                group = []
                for k in range(len(OTHERS)):
                    at = pl.multiple_of(c * CHUNK + ranks_to[k] * PIECE, PIECE)
                    cp = pltpu.make_async_remote_copy(
                        src_ref=sent1.at[pl.ds(at, PIECE)], dst_ref=parts.at[c, k],
                        send_sem=rs_send.at[c, k], recv_sem=rs_recv.at[c, k],
                        device_id=(ranks_to[k], loop), device_id_type=MESH)
                    cp.start()
                    group.append(cp)
                scatter.append(group)

        def finish(c):
            mine = pl.ds(pl.multiple_of(c * CHUNK + rep * PIECE, PIECE), PIECE)
            for cp in scatter[c]:
                cp.wait_recv()
            total = sent1[mine, :]
            for k in range(len(OTHERS)):
                total = total + parts[c, k]
            mean[c] = total * (1.0 / REPS)
            own = pltpu.make_async_copy(mean.at[c], item_out.at[mine], own_sem.at[c])
            own.start()
            outs.append(own)
            group = []
            for k in range(len(OTHERS)):
                cp = pltpu.make_async_remote_copy(
                    src_ref=mean.at[c], dst_ref=item_out.at[mine],
                    send_sem=ag_send.at[c, k], recv_sem=ag_recv.at[c, k],
                    device_id=(ranks_to[k], loop), device_id_type=MESH)
                cp.start()
                group.append(cp)
            gather.append(group)

        for u in range(N // ROWS):
            rows = pl.ds(u * ROWS, ROWS)
            d = dot(ghi[rows, :], hnew[...], NN) + dot(glo[rows, :], hnew[...], NN)
            uv[rows, :] = KEEP * uv[rows, :] + STEP * (d[:, 0:R] + d[:, R:2 * R])
            if s == 1:
                o = pltpu.make_async_copy(uv.at[rows], user_out.at[rows], out_sem.at[u])
                o.start()
                outs.append(o)
                if comm and u < CHUNKS:
                    finish(u)
    if comm:
        for cp in ring:
            cp.wait_send()
        for group in scatter:
            for cp in group:
                cp.wait_send()
        for group in gather:
            for cp in group:
                cp.wait_send()
                cp.wait_recv()
    for o in outs:
        o.wait()


def body(interactions, user_factors, item_factors, comm=True):
    n = len(OTHERS)
    return pl.pallas_call(
        functools.partial(kernel, comm),
        out_shape=[jax.ShapeDtypeStruct((N, R), F32)] * 2,
        in_specs=[pl.BlockSpec(memory_space=pl.ANY)] * 3,
        out_specs=[pl.BlockSpec(memory_space=pl.ANY)] * 2,
        scratch_shapes=[
            pltpu.VMEM((2, N, N), jnp.int32),
            pltpu.VMEM((N, R), F32),
            pltpu.VMEM((N, R), F32),
            pltpu.VMEM((N, R), F32),
            pltpu.VMEM((N, R), F32),
            pltpu.VMEM((N, R), F32),
            pltpu.VMEM((N, 2 * R), BF16),
            pltpu.VMEM((2 * R, N), BF16),
            pltpu.VMEM((CHUNK, 4 * R), BF16),
            pltpu.VMEM((N, 2 * R), BF16),
            pltpu.VMEM((N, N), BF16),
            pltpu.VMEM((N, N), BF16),
            pltpu.VMEM((CHUNKS, n, PIECE, R), F32),
            pltpu.VMEM((CHUNKS, PIECE, R), F32),
            pltpu.SemaphoreType.DMA((2,)),
            pltpu.SemaphoreType.DMA((2, CHUNKS)),
            pltpu.SemaphoreType.DMA((N // ROWS,)),
            pltpu.SemaphoreType.DMA((CHUNKS,)),
            pltpu.SemaphoreType.DMA((CHUNKS,)),
            pltpu.SemaphoreType.DMA((CHUNKS,)),
            pltpu.SemaphoreType.DMA((CHUNKS, n)),
            pltpu.SemaphoreType.DMA((CHUNKS, n)),
            pltpu.SemaphoreType.DMA((CHUNKS, n)),
            pltpu.SemaphoreType.DMA((CHUNKS, n)),
        ],
        name="sgd_window",
        compiler_params=pltpu.CompilerParams(
            collective_id=0 if comm else None, has_side_effects=True, vmem_limit_bytes=60 << 20
        ),
    )(interactions, user_factors, item_factors)


def solution(mesh):
    placed = (P(None, ("rep", "loop"), None), P(("rep", "loop"), None), P("loop", None))
    return jax.shard_map(
        body,
        mesh=mesh,
        in_specs=placed,
        out_specs=(P(("rep", "loop"), None), P("loop", None)),
        check_vma=False,
    )
```

```python
import functools

import jax
import jax.numpy as jnp
from jax import lax
from jax.experimental import pallas as pl
from jax.experimental.pallas import tpu as pltpu
from jax.sharding import PartitionSpec as P

ALPHA = 0.5
RATE = 0.01
DECAY = 0.05
KEEP = 1.0 - RATE * DECAY
STEP = RATE * ALPHA
N = 1024
R = 128
CHUNK = 256
PARTS = 2
CHUNKS = N // CHUNK
ROWS = 256
DROWS = 256
KCAT = 1
SKEW = 1
REPS = 8
PIECE = CHUNK // REPS
OTHERS = [(2, 1), (1, 1), (3, 1), (2, 0), (0, 1), (1, 0), (3, 0)]
MESH = pl.DeviceIdType.MESH
F32 = jnp.float32
BF16 = jnp.bfloat16
NT = (((1,), (1,)), ((), ()))
NN = (((1,), (0,)), ((), ()))


def split(x):
    hi = x.astype(BF16)
    return hi, (x - hi.astype(F32)).astype(BF16)


def dot(a, b, dims):
    return lax.dot_general(a, b, dims, preferred_element_type=F32)


def kernel(comm, inter, users, items, user_out, item_out, tile, uv, held0, held1, sent0, sent1,
           ucat, utcat, hpred, hnew, ghi, glo, acc, parts, mean,
           in_sem, tile_sem, out_sem, own_sem, ring_send, ring_recv, rs_send, rs_recv, ag_send, ag_recv):
    if comm:
        rep = lax.axis_index("rep")
        loop = lax.axis_index("loop")
        y, xh = rep // 2, rep % 2
        after = (rep, (loop + 1) % 32)
        before = (rep, (loop + 31) % 32)
        ranks_to = [((y + a) % 4) * 2 + (xh + b) % 2 for a, b in OTHERS]
        ranks_from = [((y + 4 - a) % 4) * 2 + (xh + b) % 2 for a, b in OTHERS]
        barrier = pltpu.get_barrier_semaphore()
        pl.semaphore_signal(barrier, inc=1, device_id=before, device_id_type=MESH)
        for k in range(len(OTHERS)):
            pl.semaphore_signal(barrier, inc=1, device_id=(ranks_from[k], loop), device_id_type=MESH)
    else:
        rep = 0

    loads = [pltpu.make_async_copy(users, uv, in_sem.at[0]), pltpu.make_async_copy(items, held0, in_sem.at[1])]
    for c in loads:
        c.start()
    tiles = []
    for s in range(2):
        for u in range(N // ROWS):
            rows = pl.ds(u * ROWS, ROWS)
            t = pltpu.make_async_copy(inter.at[s, rows], tile.at[s, rows], tile_sem.at[s, u])
            if s == 0:
                t.start()
            tiles.append(t)
    for c in loads:
        c.wait()

    ring = []
    scatter = []
    gather = []
    outs = []
    for s in range(2):
        held = held0 if s == 0 else held1
        sent = sent0 if s == 0 else sent1
        for u in range(N // ROWS):
            rows = pl.ds(u * ROWS, ROWS)
            block = uv[rows, :]
            hi, lo = split(block)
            ucat[rows, 0:R] = hi
            ucat[rows, R:2 * R] = lo

        def turn(u):
            rows = pl.ds(u * ROWS, ROWS)
            hi, lo = split(uv[rows, :].T)
            utcat[0:R, rows] = hi
            utcat[R:2 * R, rows] = lo

        def prepare(c):
            cols = pl.ds(c * CHUNK, CHUNK)
            h = held[cols, :]
            hi, lo = split(h)
            hnew[cols, 0:R] = hi
            hnew[cols, R:2 * R] = lo
            hi, lo = split(h.T)
            hpred[0:R, cols] = hi
            hpred[R:2 * R, cols] = hi
            hpred[2 * R:3 * R, cols] = lo
            hpred[3 * R:4 * R, cols] = lo

        def errors(c, u):
            cols = pl.ds(c * CHUNK, CHUNK)
            rows = pl.ds(u * ROWS, ROWS)
            uc = ucat[rows, :]
            if KCAT:
                pred = dot(jnp.concatenate([uc, uc], 1), hpred[:, cols], NN)
            else:
                pred = dot(uc, hpred[0:2 * R, cols], NN) + dot(uc, hpred[2 * R:4 * R, cols], NN)
            t = tile[s, rows, cols].astype(F32)
            hi, lo = split((1.0 / ALPHA + t) * (jnp.minimum(t, 1.0) - pred))
            ghi[rows, cols] = hi
            glo[rows, cols] = lo

        def gradient(c, u):
            cols = pl.ds(c * CHUNK, CHUNK)
            rows = pl.ds(u * DROWS, DROWS)
            ut = utcat[:, rows]
            if KCAT:
                d = dot(jnp.concatenate([ut, ut], 1), jnp.concatenate([ghi[rows, cols], glo[rows, cols]], 0), NN)
            else:
                d = dot(ut, ghi[rows, cols], NN) + dot(ut, glo[rows, cols], NN)
            if u == 0:
                acc[...] = d
            else:
                acc[...] += d

        def update(c):
            cols = pl.ds(c * CHUNK, CHUNK)
            new = KEEP * held[cols, :] + STEP * (acc[0:R, :] + acc[R:2 * R, :]).T
            sent[cols, :] = new
            if not comm:
                if s == 0:
                    held1[cols, :] = new
                else:
                    o = pltpu.make_async_copy(sent1.at[cols], item_out.at[cols], own_sem.at[c])
                    o.start()
                    outs.append(o)
                return
            if s == 0:
                if c == 0:
                    pl.semaphore_wait(barrier, 1 + len(OTHERS))
                cp = pltpu.make_async_remote_copy(
                    src_ref=sent0.at[cols], dst_ref=held1.at[cols],
                    send_sem=ring_send.at[c], recv_sem=ring_recv.at[c],
                    device_id=after, device_id_type=MESH)
                cp.start()
                ring.append(cp)
            else:
                group = []
                for k in range(len(OTHERS)):
                    at = pl.multiple_of(c * CHUNK + ranks_to[k] * PIECE, PIECE)
                    cp = pltpu.make_async_remote_copy(
                        src_ref=sent1.at[pl.ds(at, PIECE)], dst_ref=parts.at[c, k],
                        send_sem=rs_send.at[c, k], recv_sem=rs_recv.at[c, k],
                        device_id=(ranks_to[k], loop), device_id_type=MESH)
                    cp.start()
                    group.append(cp)
                scatter.append(group)

        if s == 0:
            prepare(0)
        if s == 0 and SKEW:
            for u in range(N // ROWS):
                tiles[u].wait()
                errors(0, u)
                turn(u)
            for t in tiles[N // ROWS:]:
                t.start()
            for c in range(1, CHUNKS):
                prepare(c)
                for u in range(N // ROWS):
                    errors(c, u)
                    if ROWS == DROWS:
                        gradient(c - 1, u)
                if ROWS != DROWS:
                    for u in range(N // DROWS):
                        gradient(c - 1, u)
                update(c - 1)
            for u in range(N // DROWS):
                gradient(CHUNKS - 1, u)
            update(CHUNKS - 1)
        else:
            for c in range(CHUNKS):
                if s == 1 and comm:
                    ring[c].wait_recv()
                if s == 1 or c > 0:
                    prepare(c)
                for u in range(N // ROWS):
                    if c == 0:
                        tiles[s * (N // ROWS) + u].wait()
                    errors(c, u)
                    if c == 0:
                        turn(u)
                for u in range(N // DROWS):
                    gradient(c, u)
                update(c)

        def finish(c):
            mine = pl.ds(pl.multiple_of(c * CHUNK + rep * PIECE, PIECE), PIECE)
            for cp in scatter[c]:
                cp.wait_recv()
            total = sent1[mine, :]
            for k in range(len(OTHERS)):
                total = total + parts[c, k]
            mean[c] = total * (1.0 / REPS)
            own = pltpu.make_async_copy(mean.at[c], item_out.at[mine], own_sem.at[c])
            own.start()
            outs.append(own)
            group = []
            for k in range(len(OTHERS)):
                cp = pltpu.make_async_remote_copy(
                    src_ref=mean.at[c], dst_ref=item_out.at[mine],
                    send_sem=ag_send.at[c, k], recv_sem=ag_recv.at[c, k],
                    device_id=(ranks_to[k], loop), device_id_type=MESH)
                cp.start()
                group.append(cp)
            gather.append(group)

        for u in range(N // ROWS):
            rows = pl.ds(u * ROWS, ROWS)
            d = dot(ghi[rows, :], hnew[...], NN) + dot(glo[rows, :], hnew[...], NN)
            uv[rows, :] = KEEP * uv[rows, :] + STEP * (d[:, 0:R] + d[:, R:2 * R])
            if s == 1:
                o = pltpu.make_async_copy(uv.at[rows], user_out.at[rows], out_sem.at[u])
                o.start()
                outs.append(o)
                if comm and u < CHUNKS:
                    finish(u)
    if comm:
        for cp in ring:
            cp.wait_send()
        for group in scatter:
            for cp in group:
                cp.wait_send()
        for group in gather:
            for cp in group:
                cp.wait_send()
                cp.wait_recv()
    for o in outs:
        o.wait()


def place(users, items, user_out, item_out, buf, in_sem, out_sem):
    rows = [pl.ds(p * (N // PARTS), N // PARTS) for p in range(PARTS)]
    ins, outs = [], []
    for a, src in enumerate((users, items)):
        for p in range(PARTS):
            cp = pltpu.make_async_copy(src.at[rows[p]], buf.at[a, rows[p]], in_sem.at[a, p])
            cp.start()
            ins.append(cp)
    for a, dst in enumerate((user_out, item_out)):
        for p in range(PARTS):
            ins[a * PARTS + p].wait()
            cp = pltpu.make_async_copy(buf.at[a, rows[p]], dst.at[rows[p]], out_sem.at[a, p])
            cp.start()
            outs.append(cp)
    for cp in outs:
        cp.wait()


def body(interactions, user_factors, item_factors, comm=True):
    n = len(OTHERS)
    users, items = pl.pallas_call(
        functools.partial(kernel, comm),
        out_shape=[jax.ShapeDtypeStruct((N, R), F32)] * 2,
        in_specs=[pl.BlockSpec(memory_space=pl.ANY)] * 3,
        out_specs=[pl.BlockSpec(memory_space=pl.ANY)] * 2,
        scratch_shapes=[
            pltpu.VMEM((2, N, N), jnp.int32),
            pltpu.VMEM((N, R), F32),
            pltpu.VMEM((N, R), F32),
            pltpu.VMEM((N, R), F32),
            pltpu.VMEM((N, R), F32),
            pltpu.VMEM((N, R), F32),
            pltpu.VMEM((N, 2 * R), BF16),
            pltpu.VMEM((2 * R, N), BF16),
            pltpu.VMEM((4 * R, N), BF16),
            pltpu.VMEM((N, 2 * R), BF16),
            pltpu.VMEM((N, N), BF16),
            pltpu.VMEM((N, N), BF16),
            pltpu.VMEM((2 * R, CHUNK), F32),
            pltpu.VMEM((CHUNKS, n, PIECE, R), F32),
            pltpu.VMEM((CHUNKS, PIECE, R), F32),
            pltpu.SemaphoreType.DMA((2,)),
            pltpu.SemaphoreType.DMA((2, N // ROWS)),
            pltpu.SemaphoreType.DMA((N // ROWS,)),
            pltpu.SemaphoreType.DMA((CHUNKS,)),
            pltpu.SemaphoreType.DMA((CHUNKS,)),
            pltpu.SemaphoreType.DMA((CHUNKS,)),
            pltpu.SemaphoreType.DMA((CHUNKS, n)),
            pltpu.SemaphoreType.DMA((CHUNKS, n)),
            pltpu.SemaphoreType.DMA((CHUNKS, n)),
            pltpu.SemaphoreType.DMA((CHUNKS, n)),
        ],
        name="sgd_window",
        compiler_params=pltpu.CompilerParams(
            collective_id=0 if comm else None, has_side_effects=True, vmem_limit_bytes=60 << 20
        ),
    )(interactions, user_factors, item_factors)
    if not comm:
        return users, items
    return pl.pallas_call(
        place,
        out_shape=[jax.ShapeDtypeStruct((N, R), F32)] * 2,
        in_specs=[pl.BlockSpec(memory_space=pl.ANY)] * 2,
        out_specs=[pl.BlockSpec(memory_space=pl.ANY)] * 2,
        scratch_shapes=[
            pltpu.VMEM((2, N, R), F32),
            pltpu.SemaphoreType.DMA((2, PARTS)),
            pltpu.SemaphoreType.DMA((2, PARTS)),
        ],
        name="place",
        compiler_params=pltpu.CompilerParams(vmem_limit_bytes=60 << 20),
    )(users, items)


def solution(mesh):
    placed = (P(None, ("rep", "loop"), None), P(("rep", "loop"), None), P("loop", None))
    return jax.shard_map(
        body,
        mesh=mesh,
        in_specs=placed,
        out_specs=(P(("rep", "loop"), None), P("loop", None)),
        check_vma=False,
    )
```

```python
import functools

import jax
import jax.numpy as jnp
from jax import lax
from jax.experimental import pallas as pl
from jax.experimental.pallas import tpu as pltpu
from jax.sharding import PartitionSpec as P

ALPHA = 0.5
RATE = 0.01
DECAY = 0.05
KEEP = 1.0 - RATE * DECAY
STEP = RATE * ALPHA
N = 1024
R = 128
CHUNK = 256
PARTS = 2
CHUNKS = N // CHUNK
ROWS = 256
DROWS = 256
STEPS = (2, 1, 3)
PAIRED_EARLY = [[], [], [], [(0, 0), (0, 1)]]
PAIRED_ORDER = [[], [(0, 2), (0, 3), (1, 0), (1, 1)], [], [(1, 2), (1, 3)]]
DIRECT_EARLY = [[], [], [], []]
DIRECT_ORDER = [[(2, 0)], [(2, 1)], [(2, 2)], [(2, 3)]]
KCAT = 1
SKEW = 1
REPS = 8
PIECE = CHUNK // REPS
OTHERS = [(2, 1), (1, 1), (3, 1), (2, 0), (0, 1), (1, 0), (3, 0)]
MESH = pl.DeviceIdType.MESH
F32 = jnp.float32
BF16 = jnp.bfloat16
NT = (((1,), (1,)), ((), ()))
NN = (((1,), (0,)), ((), ()))


def split(x):
    hi = x.astype(BF16)
    return hi, (x - hi.astype(F32)).astype(BF16)


def dot(a, b, dims):
    return lax.dot_general(a, b, dims, preferred_element_type=F32)


def kernel(comm, inter, users, items, user_out, item_out, tile, uv, held0, held1, sent0, sent1,
           ucat, utcat, hpred, hnew, ghi, glo, acc, parts, pairs, pair, other, mean,
           in_sem, tile_sem, out_sem, own_sem, ring_send, ring_recv, rs_send, rs_recv, x_send, x_recv, ag_send, ag_recv):
    if comm:
        rep = lax.axis_index("rep")
        loop = lax.axis_index("loop")
        y, xh = rep // 2, rep % 2
        across = (y * 2 + 1 - xh, loop)
        paired = loop // 2 % 2 == 1
        after = (rep, (loop + 1) % 32)
        before = (rep, (loop + 31) % 32)
        ranks_to = [((y + a) % 4) * 2 + (xh + b) % 2 for a, b in OTHERS]
        ranks_from = [((y + 4 - a) % 4) * 2 + (xh + b) % 2 for a, b in OTHERS]
        barrier = pltpu.get_barrier_semaphore()
        pl.semaphore_signal(barrier, inc=1, device_id=before, device_id_type=MESH)
        for k in range(len(OTHERS)):
            pl.semaphore_signal(barrier, inc=1, device_id=(ranks_from[k], loop), device_id_type=MESH)
    else:
        rep = 0

    loads = [pltpu.make_async_copy(users, uv, in_sem.at[0]), pltpu.make_async_copy(items, held0, in_sem.at[1])]
    for c in loads:
        c.start()
    tiles = []
    for s in range(2):
        for u in range(N // ROWS):
            rows = pl.ds(u * ROWS, ROWS)
            t = pltpu.make_async_copy(inter.at[s, rows], tile.at[s, rows], tile_sem.at[s, u])
            if s == 0:
                t.start()
            tiles.append(t)
    for c in loads:
        c.wait()

    ring = []
    outs = []
    def remote(src, dst, send_sem, recv_sem, to):
        return pltpu.make_async_remote_copy(
            src_ref=src, dst_ref=dst, send_sem=send_sem, recv_sem=recv_sem,
            device_id=to, device_id_type=MESH)

    def rows_of(c, i, size):
        return pl.ds(pl.multiple_of(c * CHUNK + i * size, size), size)

    def scatter(c, k):
        return remote(sent1.at[rows_of(c, ranks_to[k], PIECE)], parts.at[c, k],
                      rs_send.at[c, k], rs_recv.at[c, k], (ranks_to[k], loop))

    def gather(c, k):
        return remote(mean.at[c, pl.ds(0, PIECE)], item_out.at[rows_of(c, rep, PIECE)],
                      ag_send.at[c, k], ag_recv.at[c, k], (ranks_to[k], loop))

    def scatter_pair(c, k):
        to = (y + STEPS[k]) % 4
        return remote(sent1.at[rows_of(c, to, 2 * PIECE)], pairs.at[c, k],
                      rs_send.at[c, k], rs_recv.at[c, k], (to * 2 + xh, loop))

    def swap_pair(c):
        return remote(pair.at[c], other.at[c], x_send.at[c], x_recv.at[c], across)

    def gather_pair(c, k):
        return remote(mean.at[c], item_out.at[rows_of(c, y, 2 * PIECE)],
                      ag_send.at[c, k], ag_recv.at[c, k], ((y + STEPS[k]) % 4 * 2 + xh, loop))

    def own_pair(c):
        return pltpu.make_async_copy(mean.at[c], item_out.at[rows_of(c, y, 2 * PIECE)], own_sem.at[c])

    def own(c):
        return pltpu.make_async_copy(mean.at[c, pl.ds(0, PIECE)], item_out.at[rows_of(c, rep, PIECE)], own_sem.at[c])

    def along_y(c):
        for k in range(len(STEPS)):
            scatter_pair(c, k).wait_recv()
        total = sent1[rows_of(c, y, 2 * PIECE), :]
        for k in range(len(STEPS)):
            total = total + pairs[c, k]
        pair[c] = total
        swap_pair(c).start()

    def along_x(c):
        swap_pair(c).wait_recv()
        mean[c] = (pair[c] + other[c]) * (1.0 / REPS)
        for k in range(len(STEPS)):
            gather_pair(c, k).start()
        own_pair(c).start()

    def finish(c):
        for k in range(len(OTHERS)):
            scatter(c, k).wait_recv()
        total = sent1[rows_of(c, rep, PIECE), :]
        for k in range(len(OTHERS)):
            total = total + parts[c, k]
        mean[c, 0:PIECE] = total * (1.0 / REPS)
        for k in range(len(OTHERS)):
            gather(c, k).start()
        own(c).start()

    def go_on(pairwise, straight):
        for on, stages in ((paired, pairwise), (jnp.logical_not(paired), straight)):
            if stages:
                @pl.when(on)
                def _():
                    for stage, c in stages:
                        (along_y, along_x, finish)[stage](c)

    for s in range(2):
        held = held0 if s == 0 else held1
        sent = sent0 if s == 0 else sent1
        for u in range(N // ROWS):
            rows = pl.ds(u * ROWS, ROWS)
            block = uv[rows, :]
            hi, lo = split(block)
            ucat[rows, 0:R] = hi
            ucat[rows, R:2 * R] = lo

        def turn(u):
            rows = pl.ds(u * ROWS, ROWS)
            hi, lo = split(uv[rows, :].T)
            utcat[0:R, rows] = hi
            utcat[R:2 * R, rows] = lo

        def prepare(c):
            cols = pl.ds(c * CHUNK, CHUNK)
            h = held[cols, :]
            hi, lo = split(h)
            hnew[cols, 0:R] = hi
            hnew[cols, R:2 * R] = lo
            hi, lo = split(h.T)
            hpred[0:R, cols] = hi
            hpred[R:2 * R, cols] = hi
            hpred[2 * R:3 * R, cols] = lo
            hpred[3 * R:4 * R, cols] = lo

        def errors(c, u):
            cols = pl.ds(c * CHUNK, CHUNK)
            rows = pl.ds(u * ROWS, ROWS)
            uc = ucat[rows, :]
            if KCAT:
                pred = dot(jnp.concatenate([uc, uc], 1), hpred[:, cols], NN)
            else:
                pred = dot(uc, hpred[0:2 * R, cols], NN) + dot(uc, hpred[2 * R:4 * R, cols], NN)
            t = tile[s, rows, cols].astype(F32)
            hi, lo = split((1.0 / ALPHA + t) * (jnp.minimum(t, 1.0) - pred))
            ghi[rows, cols] = hi
            glo[rows, cols] = lo

        def gradient(c, u):
            cols = pl.ds(c * CHUNK, CHUNK)
            rows = pl.ds(u * DROWS, DROWS)
            ut = utcat[:, rows]
            if KCAT:
                d = dot(jnp.concatenate([ut, ut], 1), jnp.concatenate([ghi[rows, cols], glo[rows, cols]], 0), NN)
            else:
                d = dot(ut, ghi[rows, cols], NN) + dot(ut, glo[rows, cols], NN)
            if u == 0:
                acc[...] = d
            else:
                acc[...] += d

        def update(c):
            cols = pl.ds(c * CHUNK, CHUNK)
            new = KEEP * held[cols, :] + STEP * (acc[0:R, :] + acc[R:2 * R, :]).T
            sent[cols, :] = new
            if not comm:
                if s == 0:
                    held1[cols, :] = new
                else:
                    o = pltpu.make_async_copy(sent1.at[cols], item_out.at[cols], own_sem.at[c])
                    o.start()
                    outs.append(o)
                return
            if s == 0:
                if c == 0:
                    pl.semaphore_wait(barrier, 1 + len(OTHERS))
                cp = pltpu.make_async_remote_copy(
                    src_ref=sent0.at[cols], dst_ref=held1.at[cols],
                    send_sem=ring_send.at[c], recv_sem=ring_recv.at[c],
                    device_id=after, device_id_type=MESH)
                cp.start()
                ring.append(cp)
            else:
                @pl.when(paired)
                def _():
                    for k in range(len(STEPS)):
                        scatter_pair(c, k).start()

                @pl.when(jnp.logical_not(paired))
                def _():
                    for k in range(len(OTHERS)):
                        scatter(c, k).start()

        if s == 0:
            prepare(0)
        if s == 0 and SKEW:
            for u in range(N // ROWS):
                tiles[u].wait()
                errors(0, u)
                turn(u)
            for t in tiles[N // ROWS:]:
                t.start()
            for c in range(1, CHUNKS):
                prepare(c)
                for u in range(N // ROWS):
                    errors(c, u)
                    if ROWS == DROWS:
                        gradient(c - 1, u)
                if ROWS != DROWS:
                    for u in range(N // DROWS):
                        gradient(c - 1, u)
                update(c - 1)
            for u in range(N // DROWS):
                gradient(CHUNKS - 1, u)
            update(CHUNKS - 1)
        else:
            for c in range(CHUNKS):
                if s == 1 and comm:
                    ring[c].wait_recv()
                if s == 1 or c > 0:
                    prepare(c)
                for u in range(N // ROWS):
                    if c == 0:
                        tiles[s * (N // ROWS) + u].wait()
                    errors(c, u)
                    if c == 0:
                        turn(u)
                for u in range(N // DROWS):
                    gradient(c, u)
                update(c)
                if comm and s == 1:
                    go_on(PAIRED_EARLY[c], DIRECT_EARLY[c])

        for u in range(N // ROWS):
            rows = pl.ds(u * ROWS, ROWS)
            d = dot(ghi[rows, :], hnew[...], NN) + dot(glo[rows, :], hnew[...], NN)
            uv[rows, :] = KEEP * uv[rows, :] + STEP * (d[:, 0:R] + d[:, R:2 * R])
            if s == 1:
                o = pltpu.make_async_copy(uv.at[rows], user_out.at[rows], out_sem.at[u])
                o.start()
                outs.append(o)
                if comm:
                    go_on(PAIRED_ORDER[u], DIRECT_ORDER[u])
    if comm:
        for cp in ring:
            cp.wait_send()

        @pl.when(paired)
        def _():
            for c in range(CHUNKS):
                swap_pair(c).wait_send()
                own_pair(c).wait()
                for k in range(len(STEPS)):
                    scatter_pair(c, k).wait_send()
                    gather_pair(c, k).wait()

        @pl.when(jnp.logical_not(paired))
        def _():
            for c in range(CHUNKS):
                own(c).wait()
                for k in range(len(OTHERS)):
                    scatter(c, k).wait_send()
                    gather(c, k).wait()

    for o in outs:
        o.wait()


def place(users, items, user_out, item_out, buf, in_sem, out_sem):
    rows = [pl.ds(p * (N // PARTS), N // PARTS) for p in range(PARTS)]
    ins, outs = [], []
    for a, src in enumerate((users, items)):
        for p in range(PARTS):
            cp = pltpu.make_async_copy(src.at[rows[p]], buf.at[a, rows[p]], in_sem.at[a, p])
            cp.start()
            ins.append(cp)
    for a, dst in enumerate((user_out, item_out)):
        for p in range(PARTS):
            ins[a * PARTS + p].wait()
            cp = pltpu.make_async_copy(buf.at[a, rows[p]], dst.at[rows[p]], out_sem.at[a, p])
            cp.start()
            outs.append(cp)
    for cp in outs:
        cp.wait()


def body(interactions, user_factors, item_factors, comm=True):
    n = len(OTHERS)
    users, items = pl.pallas_call(
        functools.partial(kernel, comm),
        out_shape=[jax.ShapeDtypeStruct((N, R), F32)] * 2,
        in_specs=[pl.BlockSpec(memory_space=pl.ANY)] * 3,
        out_specs=[pl.BlockSpec(memory_space=pl.ANY)] * 2,
        scratch_shapes=[
            pltpu.VMEM((2, N, N), jnp.int32),
            pltpu.VMEM((N, R), F32),
            pltpu.VMEM((N, R), F32),
            pltpu.VMEM((N, R), F32),
            pltpu.VMEM((N, R), F32),
            pltpu.VMEM((N, R), F32),
            pltpu.VMEM((N, 2 * R), BF16),
            pltpu.VMEM((2 * R, N), BF16),
            pltpu.VMEM((4 * R, N), BF16),
            pltpu.VMEM((N, 2 * R), BF16),
            pltpu.VMEM((N, N), BF16),
            pltpu.VMEM((N, N), BF16),
            pltpu.VMEM((2 * R, CHUNK), F32),
            pltpu.VMEM((CHUNKS, n, PIECE, R), F32),
            pltpu.VMEM((CHUNKS, len(STEPS), 2 * PIECE, R), F32),
            pltpu.VMEM((CHUNKS, 2 * PIECE, R), F32),
            pltpu.VMEM((CHUNKS, 2 * PIECE, R), F32),
            pltpu.VMEM((CHUNKS, 2 * PIECE, R), F32),
            pltpu.SemaphoreType.DMA((2,)),
            pltpu.SemaphoreType.DMA((2, N // ROWS)),
            pltpu.SemaphoreType.DMA((N // ROWS,)),
            pltpu.SemaphoreType.DMA((CHUNKS,)),
            pltpu.SemaphoreType.DMA((CHUNKS,)),
            pltpu.SemaphoreType.DMA((CHUNKS,)),
            pltpu.SemaphoreType.DMA((CHUNKS, n)),
            pltpu.SemaphoreType.DMA((CHUNKS, n)),
            pltpu.SemaphoreType.DMA((CHUNKS,)),
            pltpu.SemaphoreType.DMA((CHUNKS,)),
            pltpu.SemaphoreType.DMA((CHUNKS, n)),
            pltpu.SemaphoreType.DMA((CHUNKS, n)),
        ],
        name="sgd_window",
        compiler_params=pltpu.CompilerParams(
            collective_id=0 if comm else None, has_side_effects=True, vmem_limit_bytes=60 << 20
        ),
    )(interactions, user_factors, item_factors)
    if not comm:
        return users, items
    return pl.pallas_call(
        place,
        out_shape=[jax.ShapeDtypeStruct((N, R), F32)] * 2,
        in_specs=[pl.BlockSpec(memory_space=pl.ANY)] * 2,
        out_specs=[pl.BlockSpec(memory_space=pl.ANY)] * 2,
        scratch_shapes=[
            pltpu.VMEM((2, N, R), F32),
            pltpu.SemaphoreType.DMA((2, PARTS)),
            pltpu.SemaphoreType.DMA((2, PARTS)),
        ],
        name="place",
        compiler_params=pltpu.CompilerParams(vmem_limit_bytes=60 << 20),
    )(users, items)


def solution(mesh):
    placed = (P(None, ("rep", "loop"), None), P(("rep", "loop"), None), P("loop", None))
    return jax.shard_map(
        body,
        mesh=mesh,
        in_specs=placed,
        out_specs=(P(("rep", "loop"), None), P("loop", None)),
        check_vma=False,
    )
```

```python
import functools

import jax
import jax.numpy as jnp
from jax import lax
from jax.experimental import pallas as pl
from jax.experimental.pallas import tpu as pltpu
from jax.sharding import PartitionSpec as P

ALPHA = 0.5
RATE = 0.01
DECAY = 0.05
KEEP = 1.0 - RATE * DECAY
STEP = RATE * ALPHA
N = 1024
R = 128
CHUNKS = (
    ((0, 256), (256, 256), (512, 256), (768, 256)),
    ((0, 256), (256, 256), (512, 256), (768, 256)),
)
LAST = len(CHUNKS[1])
WIDEST = 256
PARTS = 2
ROWS = 512
BLOCK = 256
STEPS = (2, 1, 3)
PAIRED_EARLY = [[], [], [], [(0, 0), (0, 1)]]
PAIRED_ORDER = [[], [(0, 2), (0, 3), (1, 0), (1, 1)], [], [(1, 2), (1, 3)]]
DIRECT_EARLY = [[], [], [], [(2, 0)]]
DIRECT_ORDER = [[(2, 1)], [(2, 2)], [(2, 3)], []]
REPS = 8
OTHERS = [(2, 1), (1, 1), (3, 1), (2, 0), (0, 1), (1, 0), (3, 0)]
MESH = pl.DeviceIdType.MESH
F32 = jnp.float32
BF16 = jnp.bfloat16
NT = (((1,), (1,)), ((), ()))
NN = (((1,), (0,)), ((), ()))


def split(x):
    hi = x.astype(BF16)
    return hi, (x - hi.astype(F32)).astype(BF16)


def dot(a, b, dims):
    return lax.dot_general(a, b, dims, preferred_element_type=F32)


def kernel(comm, inter, users, items, user_out, item_out, tile, uv, held0, held1, sent0, sent1,
           ucat, utcat, hpred, hnew, ghi, glo, acc, parts, pairs, pair, other, mean,
           in_sem, tile_sem, out_sem, own_sem, ring_send, ring_recv, rs_send, rs_recv, x_send, x_recv, ag_send, ag_recv):
    if comm:
        rep = lax.axis_index("rep")
        loop = lax.axis_index("loop")
        y, xh = rep // 2, rep % 2
        across = (y * 2 + 1 - xh, loop)
        paired = loop // 2 % 2 == 1
        after = (rep, (loop + 1) % 32)
        before = (rep, (loop + 31) % 32)
        ranks_to = [((y + a) % 4) * 2 + (xh + b) % 2 for a, b in OTHERS]
        ranks_from = [((y + 4 - a) % 4) * 2 + (xh + b) % 2 for a, b in OTHERS]
        barrier = pltpu.get_barrier_semaphore()
        pl.semaphore_signal(barrier, inc=1, device_id=before, device_id_type=MESH)
        for k in range(len(OTHERS)):
            pl.semaphore_signal(barrier, inc=1, device_id=(ranks_from[k], loop), device_id_type=MESH)
    else:
        rep = 0

    loads = [pltpu.make_async_copy(users, uv, in_sem.at[0]), pltpu.make_async_copy(items, held0, in_sem.at[1])]
    for c in loads:
        c.start()
    tiles = []
    for s in range(2):
        for u in range(N // BLOCK):
            rows = pl.ds(u * BLOCK, BLOCK)
            t = pltpu.make_async_copy(inter.at[s, rows], tile.at[s, rows], tile_sem.at[s, u])
            if s == 0:
                t.start()
            tiles.append(t)
    for c in loads:
        c.wait()

    ring = []
    outs = []
    def remote(src, dst, send_sem, recv_sem, to):
        return pltpu.make_async_remote_copy(
            src_ref=src, dst_ref=dst, send_sem=send_sem, recv_sem=recv_sem,
            device_id=to, device_id_type=MESH)

    def piece(c):
        return CHUNKS[1][c][1] // REPS

    def rows_of(c, i, size):
        return pl.ds(pl.multiple_of(CHUNKS[1][c][0] + i * size, size), size)

    def scatter(c, k):
        p = piece(c)
        return remote(sent1.at[rows_of(c, ranks_to[k], p)], parts.at[c, k, pl.ds(0, p)],
                      rs_send.at[c, k], rs_recv.at[c, k], (ranks_to[k], loop))

    def gather(c, k):
        p = piece(c)
        return remote(mean.at[c, pl.ds(0, p)], item_out.at[rows_of(c, rep, p)],
                      ag_send.at[c, k], ag_recv.at[c, k], (ranks_to[k], loop))

    def scatter_pair(c, k):
        to, p = (y + STEPS[k]) % 4, 2 * piece(c)
        return remote(sent1.at[rows_of(c, to, p)], pairs.at[c, k, pl.ds(0, p)],
                      rs_send.at[c, k], rs_recv.at[c, k], (to * 2 + xh, loop))

    def swap_pair(c):
        p = pl.ds(0, 2 * piece(c))
        return remote(pair.at[c, p], other.at[c, p], x_send.at[c], x_recv.at[c], across)

    def gather_pair(c, k):
        p = 2 * piece(c)
        return remote(mean.at[c, pl.ds(0, p)], item_out.at[rows_of(c, y, p)],
                      ag_send.at[c, k], ag_recv.at[c, k], ((y + STEPS[k]) % 4 * 2 + xh, loop))

    def own_pair(c):
        p = 2 * piece(c)
        return pltpu.make_async_copy(mean.at[c, pl.ds(0, p)], item_out.at[rows_of(c, y, p)], own_sem.at[c])

    def own(c):
        p = piece(c)
        return pltpu.make_async_copy(mean.at[c, pl.ds(0, p)], item_out.at[rows_of(c, rep, p)], own_sem.at[c])

    def along_y(c):
        for k in range(len(STEPS)):
            scatter_pair(c, k).wait_recv()
        p = 2 * piece(c)
        total = sent1[rows_of(c, y, p), :]
        for k in range(len(STEPS)):
            total = total + pairs[c, k, 0:p]
        pair[c, 0:p] = total
        swap_pair(c).start()

    def along_x(c):
        swap_pair(c).wait_recv()
        p = 2 * piece(c)
        mean[c, 0:p] = (pair[c, 0:p] + other[c, 0:p]) * (1.0 / REPS)
        for k in range(len(STEPS)):
            gather_pair(c, k).start()
        own_pair(c).start()

    def finish(c):
        for k in range(len(OTHERS)):
            scatter(c, k).wait_recv()
        p = piece(c)
        total = sent1[rows_of(c, rep, p), :]
        for k in range(len(OTHERS)):
            total = total + parts[c, k, 0:p]
        mean[c, 0:p] = total * (1.0 / REPS)
        for k in range(len(OTHERS)):
            gather(c, k).start()
        own(c).start()

    def go_on(pairwise, straight):
        for on, stages in ((paired, pairwise), (jnp.logical_not(paired), straight)):
            if stages:
                @pl.when(on)
                def _():
                    for stage, c in stages:
                        (along_y, along_x, finish)[stage](c)

    for s in range(2):
        held = held0 if s == 0 else held1
        sent = sent0 if s == 0 else sent1
        for u in range(N // BLOCK):
            rows = pl.ds(u * BLOCK, BLOCK)
            hi, lo = split(uv[rows, :])
            ucat[rows, 0:R] = hi
            ucat[rows, R:2 * R] = lo

        def turn(u):
            rows = pl.ds(u * ROWS, ROWS)
            hi, lo = split(uv[rows, :].T)
            utcat[0:R, rows] = hi
            utcat[R:2 * R, rows] = lo

        def prepare(c):
            cols = pl.ds(*CHUNKS[s][c])
            h = held[cols, :]
            hi, lo = split(h)
            hnew[cols, 0:R] = hi
            hnew[cols, R:2 * R] = lo
            hi, lo = split(h.T)
            hpred[0:R, cols] = hi
            hpred[R:2 * R, cols] = hi
            hpred[2 * R:3 * R, cols] = lo
            hpred[3 * R:4 * R, cols] = lo

        def errors(c, u):
            cols = pl.ds(*CHUNKS[s][c])
            rows = pl.ds(u * ROWS, ROWS)
            uc = ucat[rows, :]
            pred = dot(jnp.concatenate([uc, uc], 1), hpred[:, cols], NN)
            t = tile[s, rows, cols].astype(F32)
            hi, lo = split((1.0 / ALPHA + t) * (jnp.minimum(t, 1.0) - pred))
            ghi[rows, cols] = hi
            glo[rows, cols] = lo

        def gradient(c, u):
            cols = pl.ds(*CHUNKS[s][c])
            rows = pl.ds(u * ROWS, ROWS)
            ut = utcat[:, rows]
            d = dot(jnp.concatenate([ut, ut], 1), jnp.concatenate([ghi[rows, cols], glo[rows, cols]], 0), NN)
            width = CHUNKS[s][c][1]
            if u == 0:
                acc[:, 0:width] = d
            else:
                acc[:, 0:width] += d

        def update(c):
            cols = pl.ds(*CHUNKS[s][c])
            width = CHUNKS[s][c][1]
            new = KEEP * held[cols, :] + STEP * (acc[0:R, 0:width] + acc[R:2 * R, 0:width]).T
            sent[cols, :] = new
            if not comm:
                if s == 0:
                    held1[cols, :] = new
                else:
                    o = pltpu.make_async_copy(sent1.at[cols], item_out.at[cols], own_sem.at[c])
                    o.start()
                    outs.append(o)
                return
            if s == 0:
                if c == 0:
                    pl.semaphore_wait(barrier, 1 + len(OTHERS))
                first, width = CHUNKS[0][c]
                for k, (at, size) in enumerate(CHUNKS[1]):
                    if first <= at < first + width:
                        rows = pl.ds(at, size)
                        cp = remote(sent0.at[rows], held1.at[rows], ring_send.at[k], ring_recv.at[k], after)
                        cp.start()
                        ring.append(cp)
            else:
                @pl.when(paired)
                def _():
                    for k in range(len(STEPS)):
                        scatter_pair(c, k).start()

                @pl.when(jnp.logical_not(paired))
                def _():
                    for k in range(len(OTHERS)):
                        scatter(c, k).start()

        def arrive(u):
            for i in range(u * ROWS // BLOCK, (u + 1) * ROWS // BLOCK):
                tiles[s * (N // BLOCK) + i].wait()

        if s == 0:
            prepare(0)
            for u in range(N // ROWS):
                arrive(u)
                errors(0, u)
                turn(u)
            for t in tiles[N // BLOCK:]:
                t.start()
            for c in range(1, len(CHUNKS[0])):
                prepare(c)
                for u in range(N // ROWS):
                    errors(c, u)
                    gradient(c - 1, u)
                update(c - 1)
            for u in range(N // ROWS):
                gradient(len(CHUNKS[0]) - 1, u)
            update(len(CHUNKS[0]) - 1)
        else:
            for c in range(LAST):
                if comm:
                    ring[c].wait_recv()
                prepare(c)
                for u in range(N // ROWS):
                    if c == 0:
                        arrive(u)
                    errors(c, u)
                    if c == 0:
                        turn(u)
                for u in range(N // ROWS):
                    gradient(c, u)
                update(c)
                if comm:
                    go_on(PAIRED_EARLY[c], DIRECT_EARLY[c])

        for u in range(N // BLOCK):
            rows = pl.ds(u * BLOCK, BLOCK)
            d = dot(ghi[rows, :], hnew[...], NN) + dot(glo[rows, :], hnew[...], NN)
            uv[rows, :] = KEEP * uv[rows, :] + STEP * (d[:, 0:R] + d[:, R:2 * R])
            if s == 1:
                o = pltpu.make_async_copy(uv.at[rows], user_out.at[rows], out_sem.at[u])
                o.start()
                outs.append(o)
                if comm:
                    go_on(PAIRED_ORDER[u], DIRECT_ORDER[u])
    if comm:
        for cp in ring:
            cp.wait_send()

        @pl.when(paired)
        def _():
            for c in range(LAST):
                swap_pair(c).wait_send()
                own_pair(c).wait()
                for k in range(len(STEPS)):
                    scatter_pair(c, k).wait_send()
                    gather_pair(c, k).wait()

        @pl.when(jnp.logical_not(paired))
        def _():
            for c in range(LAST):
                own(c).wait()
                for k in range(len(OTHERS)):
                    scatter(c, k).wait_send()
                    gather(c, k).wait()

    for o in outs:
        o.wait()


def place(users, items, user_out, item_out, buf, in_sem, out_sem):
    rows = [pl.ds(p * (N // PARTS), N // PARTS) for p in range(PARTS)]
    ins, outs = [], []
    for a, src in enumerate((users, items)):
        for p in range(PARTS):
            cp = pltpu.make_async_copy(src.at[rows[p]], buf.at[a, rows[p]], in_sem.at[a, p])
            cp.start()
            ins.append(cp)
    for a, dst in enumerate((user_out, item_out)):
        for p in range(PARTS):
            ins[a * PARTS + p].wait()
            cp = pltpu.make_async_copy(buf.at[a, rows[p]], dst.at[rows[p]], out_sem.at[a, p])
            cp.start()
            outs.append(cp)
    for cp in outs:
        cp.wait()


def body(interactions, user_factors, item_factors, comm=True):
    n = len(OTHERS)
    users, items = pl.pallas_call(
        functools.partial(kernel, comm),
        out_shape=[jax.ShapeDtypeStruct((N, R), F32)] * 2,
        in_specs=[pl.BlockSpec(memory_space=pl.ANY)] * 3,
        out_specs=[pl.BlockSpec(memory_space=pl.ANY)] * 2,
        scratch_shapes=[
            pltpu.VMEM((2, N, N), jnp.int32),
            pltpu.VMEM((N, R), F32),
            pltpu.VMEM((N, R), F32),
            pltpu.VMEM((N, R), F32),
            pltpu.VMEM((N, R), F32),
            pltpu.VMEM((N, R), F32),
            pltpu.VMEM((N, 2 * R), BF16),
            pltpu.VMEM((2 * R, N), BF16),
            pltpu.VMEM((4 * R, N), BF16),
            pltpu.VMEM((N, 2 * R), BF16),
            pltpu.VMEM((N, N), BF16),
            pltpu.VMEM((N, N), BF16),
            pltpu.VMEM((2 * R, WIDEST), F32),
            pltpu.VMEM((LAST, n, WIDEST // REPS, R), F32),
            pltpu.VMEM((LAST, len(STEPS), 2 * WIDEST // REPS, R), F32),
            pltpu.VMEM((LAST, 2 * WIDEST // REPS, R), F32),
            pltpu.VMEM((LAST, 2 * WIDEST // REPS, R), F32),
            pltpu.VMEM((LAST, 2 * WIDEST // REPS, R), F32),
            pltpu.SemaphoreType.DMA((2,)),
            pltpu.SemaphoreType.DMA((2, N // BLOCK)),
            pltpu.SemaphoreType.DMA((N // BLOCK,)),
            pltpu.SemaphoreType.DMA((LAST,)),
            pltpu.SemaphoreType.DMA((LAST,)),
            pltpu.SemaphoreType.DMA((LAST,)),
            pltpu.SemaphoreType.DMA((LAST, n)),
            pltpu.SemaphoreType.DMA((LAST, n)),
            pltpu.SemaphoreType.DMA((LAST,)),
            pltpu.SemaphoreType.DMA((LAST,)),
            pltpu.SemaphoreType.DMA((LAST, n)),
            pltpu.SemaphoreType.DMA((LAST, n)),
        ],
        name="sgd_window",
        compiler_params=pltpu.CompilerParams(
            collective_id=0 if comm else None, has_side_effects=True, vmem_limit_bytes=60 << 20
        ),
    )(interactions, user_factors, item_factors)
    if not comm:
        return users, items
    return pl.pallas_call(
        place,
        out_shape=[jax.ShapeDtypeStruct((N, R), F32)] * 2,
        in_specs=[pl.BlockSpec(memory_space=pl.ANY)] * 2,
        out_specs=[pl.BlockSpec(memory_space=pl.ANY)] * 2,
        scratch_shapes=[
            pltpu.VMEM((2, N, R), F32),
            pltpu.SemaphoreType.DMA((2, PARTS)),
            pltpu.SemaphoreType.DMA((2, PARTS)),
        ],
        name="place",
        compiler_params=pltpu.CompilerParams(vmem_limit_bytes=60 << 20),
    )(users, items)


def solution(mesh):
    placed = (P(None, ("rep", "loop"), None), P(("rep", "loop"), None), P("loop", None))
    return jax.shard_map(
        body,
        mesh=mesh,
        in_specs=placed,
        out_specs=(P(("rep", "loop"), None), P("loop", None)),
        check_vma=False,
    )
```
